32 devices in a mesh: group: 2 (over y), fsdp: 4 (over z), seq: 2 (over x), proj: 2 (over core).
Axes of the slice: x: 2, y: 2, z: 4, core: 2. Of those that a mesh axis runs over, the one named last changes fastest.
Arguments:
- patches: bfloat16 [6144, 1280], P(('group', 'fsdp', 'seq')), parts along dimension 0, may hold values from -6 to 6
- cotangent: bfloat16 [6144, 1280], P(('group', 'fsdp', 'seq')), parts along dimension 0, may hold values from -6 to 6
- segment: int32 [6144], P(('group', 'fsdp', 'seq')), parts along dimension 0, may hold values from 0 to 7, never falling along the last dimension, each value on 1 to 768 neighbouring positions
- home_map: int32 [16], P('group'), parts along dimension 0, may hold values from 0 to 7, as said below
- ln_gain: float32 [1280], replicated, may hold values from 0.1 to 1.9
- w_up: bfloat16 [1280, 5120], P('fsdp', 'proj'), may hold values from -0.15625 to 0.15625
- w_down_t: bfloat16 [1280, 5120], P('fsdp', 'proj'), may hold values from -0.078125 to 0.078125
- p_in1: bfloat16 [1280, 32], replicated, may hold values from -0.15625 to 0.15625
- q_out1: bfloat16 [5120, 32], P('proj'), may hold values from -0.078125 to 0.078125
- p_in2: bfloat16 [5120, 32], P('proj'), may hold values from -0.078125 to 0.078125
- q_out2: bfloat16 [1280, 32], replicated, may hold values from -0.15625 to 0.15625
Outputs:
- gradients: float32 [16, 32, 64], P(('group', 'fsdp', 'seq'), 'proj'), parts along dimension 0
The draws below stay inside these ranges and needn't reach their ends.
There are 2 independent parts, one for each index of `group`. The reference program is written for one: setup_inputs(seed, part) draws one part's arguments, and reference() takes and returns one part's arrays. A program takes and returns all parts, laid end to end along the dimension named above; an argument that names none is the same for every part. Nothing has to cross between parts.
Inputs may be any that keep to these rules, and one draw needn't show every extreme that they name: segment never falls along the patches and starts at 0; every image has 1 to 768 patches and one has exactly 768. home_map is a permutation of the rows; image 0 is homed at row 4.
All inputs are finite; a program needn't handle non-finite values.
Results may differ from the reference program's by a relative error of at most 0.0055.
Values may be sent and summed in bfloat16 or wider, within the bound.
A program may use at most 64 MiB of HBM per device.

```python
import math
import jax
import jax.numpy as jnp
import numpy as np
from jax import lax

D = 1280
FF = 5120
KO = 32
KI = 32
EXAMPLES = 8
ROWS = 3072
MOST = 768


def draw_home_map(key, part):
    key = jax.random.fold_in(key, 7)
    shuffled = jax.random.permutation(key, EXAMPLES).astype(jnp.int32)
    middle = EXAMPLES // 2
    shuffled = jnp.where(shuffled == middle, shuffled[0], shuffled)
    return shuffled.at[0].set(middle).astype(jnp.int32)


def shard_levels(rng, shape, pieces, low, high):
    def one(position, shards_of):
        draws = jax.random.uniform(jax.random.fold_in(jax.random.fold_in(rng, 6), position), (shards_of,), jnp.float32, low / len(pieces), high / len(pieces))
        return jnp.repeat(jnp.exp(draws), shape[position] // shards_of).reshape((-1,) + (1,) * (len(shape) - position - 1))

    factor_of = one(*pieces[0])
    for cut in pieces[1:]:
        factor_of = factor_of * one(*cut)
    return factor_of


def length_profile(number_of, total, most, slope):
    loads = [(1 << 20) // math.isqrt(grade ** slope) + 1 for grade in range(2, number_of + 1)]
    rest, holding = total - most - (number_of - 1), [1] * (number_of - 1)
    while rest > 0:
        free = [i for i in range(number_of - 1) if holding[i] < most]
        mass, left = sum([loads[i] for i in free]), rest
        for i in free:
            addition = min(most - holding[i], max(1, left * loads[i] // mass), rest)
            holding[i] = holding[i] + addition
            rest = rest - addition
    return np.array([most] + holding)


def uneven_parts(stream_key, amount, total, most, skew):
    if amount == 2:
        one = jax.random.randint(stream_key, (), max(1, total - most), min(most, total - 1) + 1)
        return jnp.stack([one, total - one])
    tallies = jnp.asarray(length_profile(amount, total, most, skew), jnp.int32)
    couples = (amount - 1) // 2
    giver, receiver = tallies[1:1 + 2 * couples:2], tallies[2:2 + 2 * couples:2]
    margin = jnp.minimum(giver - 1, most - receiver)
    passed = jax.random.randint(jax.random.fold_in(stream_key, 1), (couples,), 0, 1 << 20) % (margin + 1)
    tallies = tallies.at[1:1 + 2 * couples:2].set(giver - passed).at[2:2 + 2 * couples:2].set(receiver + passed)
    return tallies[jax.random.permutation(jax.random.fold_in(stream_key, 2), amount)]


def bell_draw(own_key, shape, scale, limit, cuts=(), dtype=jnp.bfloat16):
    values = scale * jax.random.normal(own_key, shape, jnp.float32)
    if cuts:
        values = values * shard_levels(own_key, shape, cuts, -0.22, 0.18)
    return jnp.clip(values, -limit, limit).astype(dtype)


def setup_inputs(seed: int = 0, part: int = 0) -> dict:
    key_of = jax.random.split(jax.random.key(seed), 12)
    part_splits = jax.random.split(jax.random.fold_in(key_of[11], part), 12)
    patches = bell_draw(part_splits[0], (ROWS, D), 1.0, 6.0, ((0, 8),))
    cotangent = bell_draw(part_splits[1], (ROWS, D), 1.0, 6.0, ((0, 8),))
    segment = jnp.searchsorted(jnp.cumsum(uneven_parts(part_splits[2], EXAMPLES, ROWS, MOST, 2)), jnp.arange(ROWS), side="right").astype(jnp.int32)
    home_map = draw_home_map(jax.random.fold_in(jax.random.fold_in(key_of[11], part), 71), part)
    ln_gain = jnp.clip(1.0 + 0.18 * jax.random.normal(key_of[4], (D,), jnp.float32), 0.1, 1.9)
    w_up = bell_draw(key_of[5], (D, FF), D ** -0.5, 0.15625, ((0, 4), (1, 2)))
    w_down_t = bell_draw(key_of[6], (D, FF), FF ** -0.5, 0.078125, ((0, 4), (1, 2)))
    p_in1 = bell_draw(key_of[7], (D, KI), D ** -0.5, 0.15625)
    q_out1 = bell_draw(key_of[8], (FF, KO), FF ** -0.5, 0.078125, ((0, 2),))
    p_in2 = bell_draw(key_of[9], (FF, KI), FF ** -0.5, 0.078125, ((0, 2),))
    q_out2 = bell_draw(key_of[10], (D, KO), D ** -0.5, 0.15625)
    return dict(patches=patches, cotangent=cotangent, segment=segment, home_map=home_map, ln_gain=ln_gain, w_up=w_up, w_down_t=w_down_t, p_in1=p_in1, q_out1=q_out1, p_in2=p_in2, q_out2=q_out2)


def reference(patches, cotangent, segment, home_map, ln_gain, w_up, w_down_t, p_in1, q_out1, p_in2, q_out2):
    values = patches.astype(jnp.float32)
    center = values - lax.optimization_barrier(jnp.mean(values, axis=-1, keepdims=True))
    spread = lax.optimization_barrier(jnp.mean(center * center, axis=-1, keepdims=True))
    normed = (center * lax.rsqrt(spread + 1e-06) * ln_gain).astype(jnp.bfloat16)
    pre = jnp.dot(normed, w_up, preferred_element_type=jnp.float32)
    dact = jnp.dot(cotangent, w_down_t, preferred_element_type=jnp.float32)
    sigma = jax.nn.sigmoid(1.702 * pre)
    act = (pre * sigma).astype(jnp.bfloat16)
    dpre = (dact * (sigma + 1.702 * pre * sigma * (1.0 - sigma))).astype(jnp.bfloat16)
    in_one = jnp.dot(normed, p_in1, preferred_element_type=jnp.float32)
    out_one = jnp.dot(dpre, q_out1, preferred_element_type=jnp.float32)
    in_two = jnp.dot(act, p_in2, preferred_element_type=jnp.float32)
    out_two = jnp.dot(cotangent, q_out2, preferred_element_type=jnp.float32)
    outer = jnp.concatenate([out_one[:, :, None] * in_one[:, None, :], out_two[:, :, None] * in_two[:, None, :]], axis=2)
    target = home_map[segment].astype(jnp.int32)
    raw = jax.ops.segment_sum(outer, target, num_segments=EXAMPLES)
    counts = jax.ops.segment_sum(jnp.ones(segment.shape, jnp.float32), target, num_segments=EXAMPLES)
    return raw * lax.rsqrt(counts)[:, None, None]
```

```python
import functools

import jax
import jax.numpy as jnp
from jax import lax
from jax.experimental import pallas as pl
from jax.experimental.pallas import tpu as pltpu
from jax.sharding import PartitionSpec as P

KC = 256
HC = 128
MESH = pl.DeviceIdType.MESH
BF = jnp.bfloat16
F32 = jnp.float32
NT = (((1,), (1,)), ((), ()))


def kernel(
    fn, sn, chunks,
    patches, cot, seg, home, gain, w_up, w_down, p_in1, q_out1, p_in2, q_out2,
    out,
    pbuf, xbuf, sbuf, wbuf, p1v, q1v, p2v, q2v,
    p1p, p2p, q1t, q2t, in1, in2, t1, t2, part, gath,
    lsem, wsem, zrecv, yrecv, rsend, lsend, ysend, xsem, seg_sem, csem, red_send, red_recv,
):
    g, f = lax.axis_index("group"), lax.axis_index("fsdp")
    s, p = lax.axis_index("seq"), lax.axis_index("proj")
    s2 = lax.rem(s, 2)
    mate = s + 1 - 2 * s2
    n = fn * sn * 2
    me = (f * sn + s) * 2 + p
    rows, width = patches.shape
    half = rows // 2
    depth = w_up.shape[0]
    images = home.shape[0]
    ko = q_out1.shape[1]
    ki = p_in1.shape[1]
    cols = chunks * KC
    base = pl.multiple_of(s2 * cols, KC)

    def spot(linear):
        return {"fsdp": linear // (2 * sn), "seq": lax.rem(linear // 2, sn), "proj": lax.rem(linear, 2)}

    own_rows = pl.ds(0, rows)
    loads = [
        pltpu.make_async_copy(patches, pbuf, lsem.at[0]),
        pltpu.make_async_copy(cot, xbuf.at[1, own_rows], lsem.at[1]),
        pltpu.make_async_copy(q_out1.at[pl.ds(base, cols)], q1v, lsem.at[2]),
        pltpu.make_async_copy(p_in2.at[pl.ds(base, cols)], p2v, lsem.at[3]),
        pltpu.make_async_copy(p_in1, p1v, lsem.at[4]),
        pltpu.make_async_copy(q_out2, q2v, lsem.at[5]),
    ]

    def own_load(k, m):
        source = (w_up, w_down)[m]
        columns = pl.ds(pl.multiple_of(base + k * KC, KC), KC)
        return pltpu.make_async_copy(
            source.at[:, columns], wbuf.at[k, m, pl.ds(pl.multiple_of(f * depth, depth), depth)], wsem.at[k, m]
        )

    for k in range(chunks):
        for m in range(2):
            own_load(k, m).start()
        if k == 0:
            loads[0].start()
            loads[1].start()
    for load in loads[2:]:
        load.start()
    sbuf[0] = jnp.broadcast_to(seg[...], sbuf.shape[1:])

    barrier = pltpu.get_barrier_semaphore()

    def greet(o, carry):
        pl.semaphore_signal(barrier, inc=1, device_id=spot(lax.rem(me + o, n)), device_id_type=MESH)
        return carry

    lax.fori_loop(1, n, greet, 0)
    pl.semaphore_signal(barrier, inc=1, device_id={"group": 1 - g}, device_id_type=MESH)
    pl.semaphore_wait(barrier, n)

    def piece(k, source, side):
        return wbuf.at[
            k, :, pl.ds(pl.multiple_of(source * depth, depth), depth), pl.ds(pl.multiple_of(side * HC, HC), HC)
        ]

    def z_copy(k, source, way):
        sems = rsend if way > 0 else lsend
        block = piece(k, source, g)
        return pltpu.make_async_remote_copy(
            src_ref=block, dst_ref=block, send_sem=sems.at[k, source], recv_sem=zrecv.at[k, source],
            device_id={"fsdp": f + way}, device_id_type=MESH,
        )

    def y_copy(k, source, side):
        block = piece(k, source, side)
        return pltpu.make_async_remote_copy(
            src_ref=block, dst_ref=block, send_sem=ysend.at[k, source], recv_sem=yrecv.at[k, source],
            device_id={"group": 1 - g}, device_id_type=MESH,
        )

    def send_own(k):
        for m in range(2):
            own_load(k, m).wait()

        @pl.when(f < fn - 1)
        def _():
            z_copy(k, f, 1).start()

        @pl.when(f > 0)
        def _():
            z_copy(k, f, -1).start()

    def forward(k):
        for d in range(1, fn):
            @pl.when(f - d >= 0)
            def _():
                z_copy(k, f - d, 1).wait_recv()

                @pl.when(f < fn - 1)
                def _():
                    z_copy(k, f - d, 1).start()

                y_copy(k, f - d, g).start()

            @pl.when(f + d < fn)
            def _():
                z_copy(k, f + d, -1).wait_recv()

                @pl.when(f > 0)
                def _():
                    z_copy(k, f + d, -1).start()

                y_copy(k, f + d, g).start()

    send_own(0)
    send_own(1)

    def x_copy():
        mine = pl.ds(pl.multiple_of(p * half, half), half)
        there = pl.ds(pl.multiple_of(rows + p * half, half), half)
        return pltpu.make_async_remote_copy(
            src_ref=xbuf.at[:, mine], dst_ref=xbuf.at[:, there], send_sem=xsem.at[0], recv_sem=xsem.at[1],
            device_id={"seq": mate}, device_id_type=MESH,
        )

    def c_copy(side):
        block = xbuf.at[:, pl.ds(pl.multiple_of(rows + side * half, half), half)]
        return pltpu.make_async_remote_copy(
            src_ref=block, dst_ref=block, send_sem=csem.at[0], recv_sem=csem.at[1],
            device_id={"proj": 1 - p}, device_id_type=MESH,
        )

    seg_copy = pltpu.make_async_remote_copy(
        src_ref=sbuf.at[0], dst_ref=sbuf.at[1], send_sem=seg_sem.at[0], recv_sem=seg_sem.at[1],
        device_id={"seq": mate}, device_id_type=MESH,
    )
    seg_copy.start()

    loads[0].wait()
    step = 32

    def norm(i, carry):
        at = pl.ds(pl.multiple_of(i * step, step), step)
        values = pbuf[at, :].astype(F32)
        center = values - jnp.mean(values, axis=-1, keepdims=True)
        spread = jnp.mean(center * center, axis=-1, keepdims=True)
        xbuf[0, at, :] = (center * lax.rsqrt(spread + 1e-06) * gain[...]).astype(BF)
        return carry

    lax.fori_loop(0, rows // step, norm, 0)
    loads[1].wait()
    x_copy().start()

    for load in loads[2:]:
        load.wait()

    def pick(shape, shift):
        i = lax.broadcasted_iota(jnp.int32, shape, 0)
        j = lax.broadcasted_iota(jnp.int32, shape, 1)
        return (j == i + shift).astype(BF)

    p1p[...] = jnp.dot(p1v[...], pick((ki, 128), 0), preferred_element_type=F32).astype(BF)
    p2p[...] = jnp.dot(p2v[...], pick((ki, 128), ki), preferred_element_type=F32).astype(BF)
    eye = pick((ko, ko), 0)
    q2t[...] = lax.dot_general(eye, q2v[...], NT, preferred_element_type=F32).astype(BF)
    for k in range(chunks):
        q1t[k] = lax.dot_general(
            eye, q1v[k * KC:(k + 1) * KC, :], NT, preferred_element_type=F32
        ).astype(BF)

    def small(r):
        at = pl.ds(r * rows, rows)
        in1[r] = jnp.dot(xbuf[0, at, :], p1p[...], preferred_element_type=F32)
        t2[r] = lax.dot_general(q2t[...], xbuf[1, at, :], NT, preferred_element_type=F32)

    def compute(k):
        for d in range(1, fn):
            @pl.when(f - d >= 0)
            def _():
                y_copy(k, f - d, 1 - g).wait_recv()

            @pl.when(f + d < fn)
            def _():
                y_copy(k, f + d, 1 - g).wait_recv()

        def rows_of(r, carry):
            at = pl.ds(pl.multiple_of(r * rows, rows), rows)
            pre = jnp.dot(xbuf[0, at, :], wbuf[k, 0], preferred_element_type=F32)
            dact = jnp.dot(xbuf[1, at, :], wbuf[k, 1], preferred_element_type=F32)
            sigma = 0.5 + 0.5 * jnp.tanh(0.851 * pre)
            act = (pre * sigma).astype(BF)
            dpre = (dact * (sigma * (1.0 + 1.702 * pre * (1.0 - sigma)))).astype(BF)
            two = jnp.dot(act, p2p[k * KC:(k + 1) * KC, :], preferred_element_type=F32)
            one = lax.dot_general(q1t[k], dpre, NT, preferred_element_type=F32)
            if k == 0:
                in2[r] = two
                t1[r] = one
            else:
                in2[r] += two
                t1[r] += one
            return carry

        lax.fori_loop(0, 2, rows_of, 0)

    small(0)
    forward(0)
    send_own(2)
    forward(1)
    send_own(3)
    x_copy().wait_recv()
    c_copy(p).start()
    seg_copy.wait_recv()
    c_copy(1 - p).wait_recv()
    small(1)
    compute(0)
    forward(2)
    send_own(4)
    compute(1)
    forward(3)
    compute(2)
    forward(4)
    compute(3)
    compute(4)

    goal = []
    for r in range(2):
        ids = sbuf[r, 0:1, :]
        goal.append(lax.fori_loop(
            0, images, lambda e, t: jnp.where(ids == e, home[e], t), jnp.zeros_like(ids)
        ))
    lane = lax.broadcasted_iota(jnp.int32, (ko // 2, 128), 1)
    many = 8

    def blocks(b, carry):
        raw = jnp.zeros((many * ko, 128), F32)
        counts = [jnp.zeros((1, 1), F32) for _ in range(many)]
        for r in range(2):
            marks = [(goal[r] == b * many + j).astype(F32) for j in range(many)]
            counts = [c + jnp.sum(m, axis=1, keepdims=True) for c, m in zip(counts, marks)]
            left1 = jnp.concatenate([t1[r] * m for m in marks], axis=0)
            left2 = jnp.concatenate([t2[r] * m for m in marks], axis=0)
            raw += jnp.dot(left1, in1[r], preferred_element_type=F32, precision=lax.Precision.HIGHEST)
            raw += jnp.dot(left2, in2[r], preferred_element_type=F32, precision=lax.Precision.HIGHEST)
        for j in range(many):
            for c in range(2):
                start = j * ko + c * (ko // 2)
                part[(b * many + j) * 2 + c] = jnp.where(
                    lane == 2 * ki, counts[j], raw[start:start + ko // 2]
                )
        return carry

    lax.fori_loop(0, images // many, blocks, 0)

    def give(o):
        target = lax.rem(me + o, n)
        return pltpu.make_async_remote_copy(
            src_ref=part.at[target], dst_ref=gath.at[me], send_sem=red_send.at[target], recv_sem=red_recv.at[me],
            device_id=spot(target), device_id_type=MESH,
        )

    def take(o):
        origin = lax.rem(me + n - o, n)
        return origin, pltpu.make_async_remote_copy(
            src_ref=part.at[origin], dst_ref=gath.at[origin], send_sem=red_send.at[origin],
            recv_sem=red_recv.at[origin], device_id=spot(origin), device_id_type=MESH,
        )

    def start(o, carry):
        give(o).start()
        return carry

    lax.fori_loop(1, n, start, 0)

    def finish(o, total):
        origin, copy = take(o)
        copy.wait_recv()
        return total + gath[origin]

    total = lax.fori_loop(1, n, finish, part[me])
    out[0] = total[:, :2 * ki] * lax.rsqrt(total[:, 2 * ki:2 * ki + 1] * 0.25)

    def drain(o, carry):
        give(o).wait_send()
        return carry

    lax.fori_loop(1, n, drain, 0)
    x_copy().wait_send()
    c_copy(p).wait_send()
    seg_copy.wait_send()
    for k in range(chunks):
        @pl.when(f < fn - 1)
        def _():
            z_copy(k, f, 1).wait_send()

        @pl.when(f > 0)
        def _():
            z_copy(k, f, -1).wait_send()

        for d in range(1, fn):
            @pl.when(f - d >= 0)
            def _():
                @pl.when(f < fn - 1)
                def _():
                    z_copy(k, f - d, 1).wait_send()

                y_copy(k, f - d, g).wait_send()

            @pl.when(f + d < fn)
            def _():
                @pl.when(f > 0)
                def _():
                    z_copy(k, f + d, -1).wait_send()

                y_copy(k, f + d, g).wait_send()


def body(
    patches, cotangent, segment, home_map, ln_gain, w_up, w_down_t, p_in1, q_out1, p_in2, q_out2
):
    fn, sn = lax.axis_size("fsdp"), lax.axis_size("seq")
    n = fn * sn * 2
    rows, width = patches.shape
    cols = w_up.shape[1] // 2
    chunks = cols // KC
    ko, ki = q_out1.shape[1], p_in1.shape[1]
    any_ = pl.BlockSpec(memory_space=pl.ANY)
    vmem = pl.BlockSpec(memory_space=pltpu.VMEM)
    smem = pl.BlockSpec(memory_space=pltpu.SMEM)
    dma = pltpu.SemaphoreType.DMA
    return pl.pallas_call(
        functools.partial(kernel, fn, sn, chunks),
        out_shape=jax.ShapeDtypeStruct((1, ko // 2, 2 * ki), F32),
        in_specs=[any_, any_, vmem, smem, vmem, any_, any_, any_, any_, any_, any_],
        out_specs=vmem,
        scratch_shapes=[
            pltpu.VMEM((rows, width), BF),
            pltpu.VMEM((2, 2 * rows, width), BF),
            pltpu.VMEM((2, 8, rows), jnp.int32),
            pltpu.VMEM((chunks, 2, width, KC), BF),
            pltpu.VMEM((width, ki), BF),
            pltpu.VMEM((cols, ko), BF),
            pltpu.VMEM((cols, ki), BF),
            pltpu.VMEM((width, ko), BF),
            pltpu.VMEM((width, 128), BF),
            pltpu.VMEM((cols, 128), BF),
            pltpu.VMEM((chunks, ko, KC), BF),
            pltpu.VMEM((ko, width), BF),
            pltpu.VMEM((2, rows, 128), F32),
            pltpu.VMEM((2, rows, 128), F32),
            pltpu.VMEM((2, ko, rows), F32),
            pltpu.VMEM((2, ko, rows), F32),
            pltpu.VMEM((n, ko // 2, 128), F32),
            pltpu.VMEM((n, ko // 2, 128), F32),
            dma((6,)),
            dma((chunks, 2)),
            dma((chunks, fn)),
            dma((chunks, fn)),
            dma((chunks, fn)),
            dma((chunks, fn)),
            dma((chunks, fn)),
            dma((2,)),
            dma((2,)),
            dma((2,)),
            dma((n,)),
            dma((n,)),
        ],
        compiler_params=pltpu.CompilerParams(
            collective_id=0, has_side_effects=True, vmem_limit_bytes=48 * 1024 * 1024
        ),
    )(
        patches, cotangent, segment.reshape(1, rows), home_map, ln_gain.reshape(1, width),
        w_up, w_down_t, p_in1, q_out1, p_in2, q_out2,
    )


def solution(mesh):
    return jax.shard_map(
        body,
        mesh=mesh,
        in_specs=(
            P(("group", "fsdp", "seq"), None),
            P(("group", "fsdp", "seq"), None),
            P(("group", "fsdp", "seq")),
            P("group"),
            P(),
            P("fsdp", "proj"),
            P("fsdp", "proj"),
            P(),
            P("proj", None),
            P("proj", None),
            P(),
        ),
        out_specs=P(("group", "fsdp", "seq"), "proj", None),
        check_vma=False,
    )
```

```python
import functools

import jax
import jax.numpy as jnp
from jax import lax
from jax.experimental import pallas as pl
from jax.experimental.pallas import tpu as pltpu
from jax.sharding import PartitionSpec as P

KC = 256
HC = 128
MESH = pl.DeviceIdType.MESH
BF = jnp.bfloat16
F32 = jnp.float32
NT = (((1,), (1,)), ((), ()))


def kernel(
    fn, sn, chunks, extra,
    patches, cot, seg, home, gain, w_up, w_down, p_in1, q_out1, p_in2, q_out2,
    out,
    pbuf, xbuf, sbuf, wbuf, p1p, p2p, q1t, q2t, in1, in2, t1, t2, part, gath,
    lsem, wsem, zrecv, yrecv, rsend, lsend, ysend, xsem, esem, csem, seg_sem, red_send, red_recv,
):
    g, f = lax.axis_index("group"), lax.axis_index("fsdp")
    s, p = lax.axis_index("seq"), lax.axis_index("proj")
    s2 = lax.rem(s, 2)
    mate = s + 1 - 2 * s2
    n = fn * sn * 2
    me = (f * sn + s) * 2 + p
    rows, width = patches.shape
    half = rows // 2
    depth = w_up.shape[0]
    images = home.shape[0]
    ko = q_out1.shape[0]
    ki = p_in1.shape[0]
    cols = chunks * KC
    base = pl.multiple_of(s2 * cols, KC)

    def spot(linear):
        return {"fsdp": linear // (2 * sn), "seq": lax.rem(linear // 2, sn), "proj": lax.rem(linear, 2)}

    own_rows = pl.ds(0, rows)
    loads = [
        pltpu.make_async_copy(patches, pbuf, lsem.at[0]),
        pltpu.make_async_copy(cot, xbuf.at[1, own_rows], lsem.at[1]),
        pltpu.make_async_copy(q_out1.at[:, pl.ds(base, cols)], q1t, lsem.at[2]),
        pltpu.make_async_copy(p_in2.at[:, pl.ds(base, cols)], p2p.at[pl.ds(ki, ki)], lsem.at[3]),
        pltpu.make_async_copy(p_in1, p1p.at[pl.ds(0, ki)], lsem.at[4]),
        pltpu.make_async_copy(q_out2, q2t, lsem.at[5]),
    ]

    p1p[ki:, :] = jnp.zeros((128 - ki, width), BF)
    p2p[:ki, :] = jnp.zeros((ki, cols), BF)
    p2p[2 * ki:, :] = jnp.zeros((128 - 2 * ki, cols), BF)

    def own_load(k, m, side):
        source = (w_up, w_down)[m]
        columns = pl.ds(pl.multiple_of(base + k * KC + side * HC, HC), HC)
        return pltpu.make_async_copy(
            source.at[:, columns], wbuf.at[k, side, m, pl.ds(pl.multiple_of(f * depth, depth), depth)],
            wsem.at[k, m, side],
        )

    for k in range(chunks):
        for m in range(2):
            for side in range(2):
                own_load(k, m, side).start()
        if k == 0:
            loads[1].start()
            loads[0].start()
    for load in loads[2:]:
        load.start()
    plain = chunks - extra
    middle = jnp.logical_and(f >= 1, f <= fn - 2)
    end = jnp.logical_not(middle)
    sbuf[0] = jnp.broadcast_to(seg[...].reshape(1, rows), sbuf.shape[1:])

    barrier = pltpu.get_barrier_semaphore()

    def greet(o, carry):
        pl.semaphore_signal(barrier, inc=1, device_id=spot(lax.rem(me + o, n)), device_id_type=MESH)
        return carry

    lax.fori_loop(1, n, greet, 0)
    pl.semaphore_signal(barrier, inc=1, device_id={"group": 1 - g}, device_id_type=MESH)
    pl.semaphore_wait(barrier, n)

    steps = plain + 2 * extra

    def piece(k, source, side):
        at = pl.ds(pl.multiple_of(source * depth, depth), depth)
        if k < plain:
            return wbuf.at[k, side, :, at]
        return wbuf.at[plain, k - plain, :, at]

    def z_copy(k, source, way):
        sems = rsend if way > 0 else lsend
        block = piece(k, source, g)
        return pltpu.make_async_remote_copy(
            src_ref=block, dst_ref=block, send_sem=sems.at[k, source], recv_sem=zrecv.at[k, source],
            device_id={"fsdp": f + way}, device_id_type=MESH,
        )

    def y_copy(k, source, side):
        block = piece(k, source, side)
        return pltpu.make_async_remote_copy(
            src_ref=block, dst_ref=block, send_sem=ysend.at[k, source], recv_sem=yrecv.at[k, source],
            device_id={"group": 1 - g}, device_id_type=MESH,
        )

    def to_right(k):
        return f < (fn - 1 if k < plain else fn - 2)

    def to_left(k):
        return f > (0 if k < plain else 1)

    def got(k, d):
        left, right = f - d >= 0, f + d < fn
        if k >= plain:
            left, right = jnp.logical_and(left, middle), jnp.logical_and(right, middle)
        return left, right

    def send_own(k):
        if k < plain or k == plain:
            for m in range(2):
                for side in range(2):
                    own_load(min(k, plain), m, side).wait()

        @pl.when(to_right(k))
        def _():
            z_copy(k, f, 1).start()

        @pl.when(to_left(k))
        def _():
            z_copy(k, f, -1).start()

    def forward(k):
        for d in range(1, fn):
            left, right = got(k, d)

            @pl.when(left)
            def _():
                z_copy(k, f - d, 1).wait_recv()

                @pl.when(to_right(k))
                def _():
                    z_copy(k, f - d, 1).start()

                if k < plain:
                    y_copy(k, f - d, g).start()

            @pl.when(right)
            def _():
                z_copy(k, f + d, -1).wait_recv()

                @pl.when(to_left(k))
                def _():
                    z_copy(k, f + d, -1).start()

                if k < plain:
                    y_copy(k, f + d, g).start()

    def half_of(m, block, side):
        return xbuf.at[m, pl.ds(pl.multiple_of(block * rows + side * half, half), half)]

    def x_copy(m, block):
        return pltpu.make_async_remote_copy(
            src_ref=half_of(m, block, p), dst_ref=half_of(m, block + 1, p),
            send_sem=xsem.at[0, m, block], recv_sem=xsem.at[1, m, block],
            device_id={"seq": mate}, device_id_type=MESH,
        )

    def c_copy(m, block, side):
        return pltpu.make_async_remote_copy(
            src_ref=half_of(m, block, side), dst_ref=half_of(m, block, side),
            send_sem=csem.at[0, m, block], recv_sem=csem.at[1, m, block],
            device_id={"proj": 1 - p}, device_id_type=MESH,
        )

    inward = jnp.where(f == 0, 1, fn - 2)

    def e_copy(m):
        return pltpu.make_async_remote_copy(
            src_ref=half_of(m, 0, p), dst_ref=half_of(m, 2, p), send_sem=esem.at[0, m], recv_sem=esem.at[1, m],
            device_id={"fsdp": inward}, device_id_type=MESH,
        )

    def seg_copy(source, target, where):
        return pltpu.make_async_remote_copy(
            src_ref=sbuf.at[source], dst_ref=sbuf.at[target], send_sem=seg_sem.at[0, target],
            recv_sem=seg_sem.at[1, target], device_id=where, device_id_type=MESH,
        )

    across = {"seq": mate}
    send_own(0)
    loads[1].wait()
    x_copy(1, 0).start()
    seg_copy(0, 1, across).start()
    if extra:
        @pl.when(end)
        def _():
            e_copy(1).start()
            seg_copy(0, 2, {"fsdp": inward}).start()

    send_own(1)
    loads[0].wait()
    step = 32
    scale = gain[...].reshape(1, width)

    def norm(i, carry):
        at = pl.ds(pl.multiple_of(i * step, step), step)
        values = pbuf[at, :].astype(F32)
        center = values - jnp.mean(values, axis=-1, keepdims=True)
        spread = jnp.mean(center * center, axis=-1, keepdims=True)
        xbuf[0, at, :] = (center * lax.rsqrt(spread + 1e-06) * scale).astype(BF)
        return carry

    lax.fori_loop(0, rows // step, norm, 0)
    x_copy(0, 0).start()
    if extra:
        @pl.when(end)
        def _():
            e_copy(0).start()

    for load in loads[2:]:
        load.wait()

    def small(r):
        at = pl.ds(r * rows, rows)
        in1[r] = lax.dot_general(xbuf[0, at, :], p1p[...], NT, preferred_element_type=F32)
        t2[r] = lax.dot_general(q2t[...], xbuf[1, at, :], NT, preferred_element_type=F32)

    def compute(k, low, high):
        for d in range(1, fn if k < plain else 1):
            @pl.when(f - d >= 0)
            def _():
                y_copy(k, f - d, 1 - g).wait_recv()

            @pl.when(f + d < fn)
            def _():
                y_copy(k, f + d, 1 - g).wait_recv()

        def rows_of(r, carry):
            at = pl.ds(pl.multiple_of(r * rows, rows), rows)
            up = jnp.concatenate([wbuf[k, 0, 0], wbuf[k, 1, 0]], axis=1)
            down = jnp.concatenate([wbuf[k, 0, 1], wbuf[k, 1, 1]], axis=1)
            pre = jnp.dot(xbuf[0, at, :], up, preferred_element_type=F32)
            dact = jnp.dot(xbuf[1, at, :], down, preferred_element_type=F32)
            sigma = 0.5 + 0.5 * jnp.tanh(0.851 * pre)
            act = (pre * sigma).astype(BF)
            dpre = (dact * (sigma * (1.0 + 1.702 * pre * (1.0 - sigma)))).astype(BF)
            two = lax.dot_general(act, p2p[:, k * KC:(k + 1) * KC], NT, preferred_element_type=F32)
            one = lax.dot_general(q1t[:, k * KC:(k + 1) * KC], dpre, NT, preferred_element_type=F32)
            if k == 0 or low == 2:
                in2[r] = two
                t1[r] = one
            else:
                in2[r] += two
                t1[r] += one
            return carry

        lax.fori_loop(low, high, rows_of, 0)

    def hand_on(m, block):
        c_copy(m, block, p).start()

    def from_end(m):
        if extra:
            @pl.when(middle)
            def _():
                e_copy(m).wait_recv()
                x_copy(m, 2).start()
                hand_on(m, 2)

    small(0)
    forward(0)
    send_own(2)
    forward(1)
    send_own(3)
    x_copy(1, 0).wait_recv()
    hand_on(1, 1)
    from_end(1)
    x_copy(0, 0).wait_recv()
    hand_on(0, 1)
    seg_copy(0, 1, across).wait_recv()
    c_copy(1, 1, 1 - p).wait_recv()
    c_copy(0, 1, 1 - p).wait_recv()
    if extra:
        @pl.when(middle)
        def _():
            seg_copy(0, 2, {"fsdp": inward}).wait_recv()
            seg_copy(2, 3, across).start()

    small(1)
    for k in range(2, steps):
        if k == 2:
            from_end(0)
        forward(k)
        if k + 2 < steps:
            send_own(k + 2)
        if k - 2 < plain - 1:
            compute(k - 2, 0, 2)
    for k in range(steps - 2, plain):
        compute(k, 0, 2)
    if extra:
        @pl.when(middle)
        def _():
            for m in (1, 0):
                x_copy(m, 2).wait_recv()
                hand_on(m, 3)

        compute(plain - 1, 0, 2)

        @pl.when(middle)
        def _():
            compute(plain, 0, 2)
            seg_copy(2, 3, across).wait_recv()
            for block in (2, 3):
                for m in (1, 0):
                    c_copy(m, block, 1 - p).wait_recv()
                small(block)
            compute(plain, 2, 4)

    lane = lax.broadcasted_iota(jnp.int32, (ko // 2, 128), 1)
    many = 8

    def blocks(b, carry):
        def add(r, sums):
            raw, counts = sums
            ids = sbuf[r, 0:1, :]
            goal = lax.fori_loop(
                0, images, lambda e, t: jnp.where(ids == e, home[e], t), jnp.zeros_like(ids), unroll=images <= 8
            )
            marks = [(goal == b * many + j).astype(F32) for j in range(many)]
            own = (r < 2).astype(F32)
            counts = tuple(c + own * jnp.sum(m, axis=1, keepdims=True) for c, m in zip(counts, marks))
            left1 = jnp.concatenate([t1[r] * m for m in marks], axis=0)
            left2 = jnp.concatenate([t2[r] * m for m in marks], axis=0)
            raw += jnp.dot(left1, in1[r], preferred_element_type=F32, precision=lax.Precision.HIGHEST)
            raw += jnp.dot(left2, in2[r], preferred_element_type=F32, precision=lax.Precision.HIGHEST)
            return raw, counts

        blank = (jnp.zeros((many * ko, 128), F32), (jnp.zeros((1, 1), F32),) * many)
        raw, counts = lax.fori_loop(0, jnp.where(middle, 4, 2) if extra else 2, add, blank)
        for j in range(many):
            for c in range(2):
                start = j * ko + c * (ko // 2)
                part[(b * many + j) * 2 + c] = jnp.where(
                    lane == 2 * ki, counts[j], raw[start:start + ko // 2]
                )
        return carry

    lax.fori_loop(0, images // many, blocks, 0)

    def give(o):
        target = lax.rem(me + o, n)
        return pltpu.make_async_remote_copy(
            src_ref=part.at[target], dst_ref=gath.at[me], send_sem=red_send.at[target], recv_sem=red_recv.at[me],
            device_id=spot(target), device_id_type=MESH,
        )

    def take(o):
        origin = lax.rem(me + n - o, n)
        return origin, pltpu.make_async_remote_copy(
            src_ref=part.at[origin], dst_ref=gath.at[origin], send_sem=red_send.at[origin],
            recv_sem=red_recv.at[origin], device_id=spot(origin), device_id_type=MESH,
        )

    def start(o, carry):
        give(o).start()
        return carry

    lax.fori_loop(1, n, start, 0)

    def finish(o, total):
        origin, copy = take(o)
        copy.wait_recv()
        return total + gath[origin]

    total = lax.fori_loop(1, n, finish, part[me])
    out[0] = total[:, :2 * ki] * lax.rsqrt(total[:, 2 * ki:2 * ki + 1] * 0.25)

    def drain(o, carry):
        give(o).wait_send()
        return carry

    lax.fori_loop(1, n, drain, 0)
    for m in range(2):
        x_copy(m, 0).wait_send()
        c_copy(m, 1, p).wait_send()
    seg_copy(0, 1, across).wait_send()
    if extra:
        @pl.when(end)
        def _():
            for m in range(2):
                e_copy(m).wait_send()
            seg_copy(0, 2, {"fsdp": inward}).wait_send()

        @pl.when(middle)
        def _():
            for m in range(2):
                x_copy(m, 2).wait_send()
                c_copy(m, 2, p).wait_send()
                c_copy(m, 3, p).wait_send()
            seg_copy(2, 3, across).wait_send()

    for k in range(steps):
        @pl.when(to_right(k))
        def _():
            z_copy(k, f, 1).wait_send()

        @pl.when(to_left(k))
        def _():
            z_copy(k, f, -1).wait_send()

        for d in range(1, fn):
            left, right = got(k, d)

            @pl.when(left)
            def _():
                @pl.when(to_right(k))
                def _():
                    z_copy(k, f - d, 1).wait_send()

                if k < plain:
                    y_copy(k, f - d, g).wait_send()

            @pl.when(right)
            def _():
                @pl.when(to_left(k))
                def _():
                    z_copy(k, f + d, -1).wait_send()

                if k < plain:
                    y_copy(k, f + d, g).wait_send()


def body(
    patches, cotangent, segment, home_map, ln_gain, w_up, w_down_t, p_in1, q_out1, p_in2, q_out2
):
    fn, sn = lax.axis_size("fsdp"), lax.axis_size("seq")
    n = fn * sn * 2
    rows, width = patches.shape
    cols = w_up.shape[1] // 2
    chunks = cols // KC
    extra = 1 if fn == 4 else 0
    blocks = 2 + 2 * extra
    steps = chunks + extra
    ko, ki = q_out1.shape[1], p_in1.shape[1]
    any_ = pl.BlockSpec(memory_space=pltpu.HBM)
    vmem = pl.BlockSpec(memory_space=pltpu.VMEM)
    smem = pl.BlockSpec(memory_space=pltpu.SMEM)
    dma = pltpu.SemaphoreType.DMA
    return pl.pallas_call(
        functools.partial(kernel, fn, sn, chunks, extra),
        out_shape=jax.ShapeDtypeStruct((1, ko // 2, 2 * ki), F32),
        in_specs=[any_, any_, vmem, smem, vmem, any_, any_, any_, any_, any_, any_],
        out_specs=vmem,
        scratch_shapes=[
            pltpu.VMEM((rows, width), BF),
            pltpu.VMEM((2, blocks * rows, width), BF),
            pltpu.VMEM((blocks, 8, rows), jnp.int32),
            pltpu.VMEM((chunks, 2, 2, width, HC), BF),
            pltpu.VMEM((128, width), BF),
            pltpu.VMEM((128, cols), BF),
            pltpu.VMEM((ko, cols), BF),
            pltpu.VMEM((ko, width), BF),
            pltpu.VMEM((blocks, rows, 128), F32),
            pltpu.VMEM((blocks, rows, 128), F32),
            pltpu.VMEM((blocks, ko, rows), F32),
            pltpu.VMEM((blocks, ko, rows), F32),
            pltpu.VMEM((n, ko // 2, 128), F32),
            pltpu.VMEM((n, ko // 2, 128), F32),
            dma((6,)),
            dma((chunks, 2, 2)),
            dma((steps, fn)),
            dma((steps, fn)),
            dma((steps, fn)),
            dma((steps, fn)),
            dma((steps, fn)),
            dma((2, 2, blocks)),
            dma((2, 2)),
            dma((2, 2, blocks)),
            dma((2, blocks)),
            dma((n,)),
            dma((n,)),
        ],
        compiler_params=pltpu.CompilerParams(
            collective_id=0, has_side_effects=True, vmem_limit_bytes=63 * 1024 * 1024
        ),
    )(
        patches, cotangent, segment, home_map, ln_gain,
        w_up, w_down_t, p_in1.T, q_out1.T, p_in2.T, q_out2.T,
    )


def solution(mesh):
    return jax.shard_map(
        body,
        mesh=mesh,
        in_specs=(
            P(("group", "fsdp", "seq"), None),
            P(("group", "fsdp", "seq"), None),
            P(("group", "fsdp", "seq")),
            P("group"),
            P(),
            P("fsdp", "proj"),
            P("fsdp", "proj"),
            P(),
            P("proj", None),
            P("proj", None),
            P(),
        ),
        out_specs=P(("group", "fsdp", "seq"), "proj", None),
        check_vma=False,
    )
```

```python
import functools

import jax
import jax.numpy as jnp
from jax import lax
from jax.experimental import pallas as pl
from jax.experimental.pallas import tpu as pltpu
from jax.sharding import PartitionSpec as P

KC = 256
HC = 128
MESH = pl.DeviceIdType.MESH
BF = jnp.bfloat16
F32 = jnp.float32
NT = (((1,), (1,)), ((), ()))


def kernel(
    fn, sn, chunks, extra,
    patches, cot, seg, home, gain, w_up, w_down, p_in1, q_out1, p_in2, q_out2,
    out,
    pbuf, xbuf, sbuf, wbuf, p1p, p2p, q1t, q2t, in1, in2, t1, t2, part, gath,
    lsem, wsem, zrecv, yrecv, rsend, lsend, ysend, xsem, esem, csem, seg_sem, red_send, red_recv,
):
    g, f = lax.axis_index("group"), lax.axis_index("fsdp")
    s, p = lax.axis_index("seq"), lax.axis_index("proj")
    s2 = lax.rem(s, 2)
    mate = s + 1 - 2 * s2
    n = fn * sn * 2
    me = (f * sn + s) * 2 + p
    rows, width = patches.shape
    half = rows // 2
    depth = w_up.shape[0]
    images = home.shape[0]
    ko = q_out1.shape[0]
    ki = p_in1.shape[0]
    cols = chunks * KC
    base = pl.multiple_of(s2 * cols, KC)

    def spot(linear):
        return {"fsdp": linear // (2 * sn), "seq": lax.rem(linear // 2, sn), "proj": lax.rem(linear, 2)}

    barrier = pltpu.get_barrier_semaphore()

    def greet(o, carry):
        pl.semaphore_signal(barrier, inc=1, device_id=spot(lax.rem(me + o, n)), device_id_type=MESH)
        return carry

    lax.fori_loop(1, n, greet, 0)
    pl.semaphore_signal(barrier, inc=1, device_id={"group": 1 - g}, device_id_type=MESH)

    own_rows = pl.ds(0, rows)
    loads = [
        pltpu.make_async_copy(patches, pbuf, lsem.at[0]),
        pltpu.make_async_copy(cot, xbuf.at[1, own_rows], lsem.at[1]),
        pltpu.make_async_copy(q_out1.at[:, pl.ds(base, cols)], q1t, lsem.at[2]),
        pltpu.make_async_copy(p_in2.at[:, pl.ds(base, cols)], p2p.at[pl.ds(ki, ki)], lsem.at[3]),
        pltpu.make_async_copy(p_in1, p1p.at[pl.ds(0, ki)], lsem.at[4]),
        pltpu.make_async_copy(q_out2, q2t, lsem.at[5]),
    ]

    p1p[ki:, :] = jnp.zeros((128 - ki, width), BF)
    p2p[:ki, :] = jnp.zeros((ki, cols), BF)
    p2p[2 * ki:, :] = jnp.zeros((128 - 2 * ki, cols), BF)

    def own_load(k, m, side):
        source = (w_up, w_down)[m]
        columns = pl.ds(pl.multiple_of(base + k * KC + side * HC, HC), HC)
        return pltpu.make_async_copy(
            source.at[:, columns], wbuf.at[k, side, m, pl.ds(pl.multiple_of(f * depth, depth), depth)],
            wsem.at[k, m, side],
        )

    for k in range(chunks):
        for m in range(2):
            for side in range(2):
                own_load(k, m, side).start()
        if k == 0:
            loads[1].start()
            loads[0].start()
    for load in loads[2:]:
        load.start()
    plain = chunks - extra
    middle = jnp.logical_and(f >= 1, f <= fn - 2)
    end = jnp.logical_not(middle)
    sbuf[0] = jnp.broadcast_to(seg[...].reshape(1, rows), sbuf.shape[1:])

    pl.semaphore_wait(barrier, n)

    steps = plain + 2 * extra

    def piece(k, source, side):
        at = pl.ds(pl.multiple_of(source * depth, depth), depth)
        if k < plain:
            return wbuf.at[k, side, :, at]
        return wbuf.at[plain, k - plain, :, at]

    def z_copy(k, source, way):
        sems = rsend if way > 0 else lsend
        block = piece(k, source, g)
        return pltpu.make_async_remote_copy(
            src_ref=block, dst_ref=block, send_sem=sems.at[k, source], recv_sem=zrecv.at[k, source],
            device_id={"fsdp": f + way}, device_id_type=MESH,
        )

    def y_copy(k, source, side):
        block = piece(k, source, side)
        return pltpu.make_async_remote_copy(
            src_ref=block, dst_ref=block, send_sem=ysend.at[k, source], recv_sem=yrecv.at[k, source],
            device_id={"group": 1 - g}, device_id_type=MESH,
        )

    def to_right(k):
        return f < (fn - 1 if k < plain else fn - 2)

    def to_left(k):
        return f > (0 if k < plain else 1)

    def got(k, d):
        left, right = f - d >= 0, f + d < fn
        if k >= plain:
            left, right = jnp.logical_and(left, middle), jnp.logical_and(right, middle)
        return left, right

    def send_own(k):
        if k < plain or k == plain:
            for m in range(2):
                for side in range(2):
                    own_load(min(k, plain), m, side).wait()

        @pl.when(to_right(k))
        def _():
            z_copy(k, f, 1).start()

        @pl.when(to_left(k))
        def _():
            z_copy(k, f, -1).start()

    def forward(k):
        for d in range(1, fn):
            left, right = got(k, d)

            @pl.when(left)
            def _():
                z_copy(k, f - d, 1).wait_recv()

                @pl.when(to_right(k))
                def _():
                    z_copy(k, f - d, 1).start()

                if k < plain:
                    y_copy(k, f - d, g).start()

            @pl.when(right)
            def _():
                z_copy(k, f + d, -1).wait_recv()

                @pl.when(to_left(k))
                def _():
                    z_copy(k, f + d, -1).start()

                if k < plain:
                    y_copy(k, f + d, g).start()

    def half_of(m, block, side):
        return xbuf.at[m, pl.ds(pl.multiple_of(block * rows + side * half, half), half)]

    def x_copy(m, block):
        return pltpu.make_async_remote_copy(
            src_ref=half_of(m, block, p), dst_ref=half_of(m, block + 1, p),
            send_sem=xsem.at[0, m, block], recv_sem=xsem.at[1, m, block],
            device_id={"seq": mate}, device_id_type=MESH,
        )

    def c_copy(m, block, side):
        return pltpu.make_async_remote_copy(
            src_ref=half_of(m, block, side), dst_ref=half_of(m, block, side),
            send_sem=csem.at[0, m, block], recv_sem=csem.at[1, m, block],
            device_id={"proj": 1 - p}, device_id_type=MESH,
        )

    inward = jnp.where(f == 0, 1, fn - 2)

    def e_copy(m):
        return pltpu.make_async_remote_copy(
            src_ref=half_of(m, 0, p), dst_ref=half_of(m, 2, p), send_sem=esem.at[0, m], recv_sem=esem.at[1, m],
            device_id={"fsdp": inward}, device_id_type=MESH,
        )

    def seg_copy(source, target, where):
        return pltpu.make_async_remote_copy(
            src_ref=sbuf.at[source], dst_ref=sbuf.at[target], send_sem=seg_sem.at[0, target],
            recv_sem=seg_sem.at[1, target], device_id=where, device_id_type=MESH,
        )

    across = {"seq": mate}
    send_own(0)
    loads[1].wait()
    x_copy(1, 0).start()
    seg_copy(0, 1, across).start()
    if extra:
        @pl.when(end)
        def _():
            e_copy(1).start()
            seg_copy(0, 2, {"fsdp": inward}).start()

    send_own(1)
    loads[0].wait()
    step = 32
    scale = gain[...].reshape(1, width)

    def norm(i, carry):
        at = pl.ds(pl.multiple_of(i * step, step), step)
        values = pbuf[at, :].astype(F32)
        center = values - jnp.mean(values, axis=-1, keepdims=True)
        spread = jnp.mean(center * center, axis=-1, keepdims=True)
        xbuf[0, at, :] = (center * lax.rsqrt(spread + 1e-06) * scale).astype(BF)
        return carry

    lax.fori_loop(0, rows // step, norm, 0)
    x_copy(0, 0).start()
    if extra:
        @pl.when(end)
        def _():
            e_copy(0).start()

    for load in loads[2:]:
        load.wait()

    def small(r):
        at = pl.ds(r * rows, rows)
        in1[r] = lax.dot_general(xbuf[0, at, :], p1p[...], NT, preferred_element_type=F32)
        t2[r] = lax.dot_general(q2t[...], xbuf[1, at, :], NT, preferred_element_type=F32)

    def compute(k, low, high):
        for d in range(1, fn if k < plain else 1):
            @pl.when(f - d >= 0)
            def _():
                y_copy(k, f - d, 1 - g).wait_recv()

            @pl.when(f + d < fn)
            def _():
                y_copy(k, f + d, 1 - g).wait_recv()

        def rows_of(r, carry):
            at = pl.ds(pl.multiple_of(r * rows, rows), rows)
            up = jnp.concatenate([wbuf[k, 0, 0], wbuf[k, 1, 0]], axis=1)
            down = jnp.concatenate([wbuf[k, 0, 1], wbuf[k, 1, 1]], axis=1)
            pre = jnp.dot(xbuf[0, at, :], up, preferred_element_type=F32)
            dact = jnp.dot(xbuf[1, at, :], down, preferred_element_type=F32)
            sigma = 0.5 + 0.5 * jnp.tanh(0.851 * pre)
            act = (pre * sigma).astype(BF)
            dpre = (dact * (sigma * (1.0 + 1.702 * pre * (1.0 - sigma)))).astype(BF)
            two = lax.dot_general(act, p2p[:, k * KC:(k + 1) * KC], NT, preferred_element_type=F32)
            one = lax.dot_general(q1t[:, k * KC:(k + 1) * KC], dpre, NT, preferred_element_type=F32)
            if k == 0 or low >= 2:
                in2[r] = two
                t1[r] = one
            else:
                in2[r] += two
                t1[r] += one
            return carry

        lax.fori_loop(low, high, rows_of, 0)

    def hand_on(m, block):
        c_copy(m, block, p).start()

    def from_end(m):
        if extra:
            @pl.when(middle)
            def _():
                e_copy(m).wait_recv()
                x_copy(m, 2).start()
                hand_on(m, 2)

    small(0)
    forward(0)
    send_own(2)
    forward(1)
    send_own(3)
    x_copy(1, 0).wait_recv()
    hand_on(1, 1)
    from_end(1)
    x_copy(0, 0).wait_recv()
    hand_on(0, 1)
    seg_copy(0, 1, across).wait_recv()
    c_copy(1, 1, 1 - p).wait_recv()
    c_copy(0, 1, 1 - p).wait_recv()
    if extra:
        @pl.when(middle)
        def _():
            seg_copy(0, 2, {"fsdp": inward}).wait_recv()
            seg_copy(2, 3, across).start()

    small(1)
    for k in range(2, steps):
        if k == 2:
            from_end(0)
        forward(k)
        if k + 2 < steps:
            send_own(k + 2)
        if k - 2 < plain - 1:
            compute(k - 2, 0, 2)
    for k in range(steps - 2, plain):
        compute(k, 0, 2)
    if extra:
        compute(plain - 1, 0, 2)

        @pl.when(middle)
        def _():
            for m in (1, 0):
                c_copy(m, 2, 1 - p).wait_recv()
            small(2)
            for m in (1, 0):
                x_copy(m, 2).wait_recv()
                hand_on(m, 3)
            compute(plain, 0, 2)
            compute(plain, 2, 3)
            seg_copy(2, 3, across).wait_recv()
            for m in (1, 0):
                c_copy(m, 3, 1 - p).wait_recv()
            small(3)
            compute(plain, 3, 4)

    lane = lax.broadcasted_iota(jnp.int32, (ko // 2, 128), 1)
    many = 8

    def blocks(b, carry):
        def add(r, sums):
            raw, counts = sums
            ids = sbuf[r, 0:1, :]
            goal = lax.fori_loop(
                0, images, lambda e, t: jnp.where(ids == e, home[e], t), jnp.zeros_like(ids), unroll=images <= 8
            )
            marks = [(goal == b * many + j).astype(F32) for j in range(many)]
            own = (r < 2).astype(F32)
            counts = tuple(c + own * jnp.sum(m, axis=1, keepdims=True) for c, m in zip(counts, marks))
            left1 = jnp.concatenate([t1[r] * m for m in marks], axis=0)
            left2 = jnp.concatenate([t2[r] * m for m in marks], axis=0)
            raw += jnp.dot(left1, in1[r], preferred_element_type=F32, precision=lax.Precision.HIGHEST)
            raw += jnp.dot(left2, in2[r], preferred_element_type=F32, precision=lax.Precision.HIGHEST)
            return raw, counts

        blank = (jnp.zeros((many * ko, 128), F32), (jnp.zeros((1, 1), F32),) * many)
        raw, counts = lax.fori_loop(0, jnp.where(middle, 4, 2) if extra else 2, add, blank)
        for j in range(many):
            for c in range(2):
                start = j * ko + c * (ko // 2)
                part[(b * many + j) * 2 + c] = jnp.where(
                    lane == 2 * ki, counts[j], raw[start:start + ko // 2]
                )
        return carry

    lax.fori_loop(0, images // many, blocks, 0)

    def give(o):
        target = lax.rem(me + o, n)
        return pltpu.make_async_remote_copy(
            src_ref=part.at[target], dst_ref=gath.at[me], send_sem=red_send.at[target], recv_sem=red_recv.at[me],
            device_id=spot(target), device_id_type=MESH,
        )

    def take(o):
        origin = lax.rem(me + n - o, n)
        return origin, pltpu.make_async_remote_copy(
            src_ref=part.at[origin], dst_ref=gath.at[origin], send_sem=red_send.at[origin],
            recv_sem=red_recv.at[origin], device_id=spot(origin), device_id_type=MESH,
        )

    def start(o, carry):
        give(o).start()
        return carry

    lax.fori_loop(1, n, start, 0)

    for m in range(2):
        x_copy(m, 0).wait_send()
        c_copy(m, 1, p).wait_send()
    seg_copy(0, 1, across).wait_send()
    if extra:
        @pl.when(end)
        def _():
            for m in range(2):
                e_copy(m).wait_send()
            seg_copy(0, 2, {"fsdp": inward}).wait_send()

        @pl.when(middle)
        def _():
            for m in range(2):
                x_copy(m, 2).wait_send()
                c_copy(m, 2, p).wait_send()
                c_copy(m, 3, p).wait_send()
            seg_copy(2, 3, across).wait_send()

    for k in range(steps):
        @pl.when(to_right(k))
        def _():
            z_copy(k, f, 1).wait_send()

        @pl.when(to_left(k))
        def _():
            z_copy(k, f, -1).wait_send()

        for d in range(1, fn):
            left, right = got(k, d)

            @pl.when(left)
            def _():
                @pl.when(to_right(k))
                def _():
                    z_copy(k, f - d, 1).wait_send()

                if k < plain:
                    y_copy(k, f - d, g).wait_send()

            @pl.when(right)
            def _():
                @pl.when(to_left(k))
                def _():
                    z_copy(k, f + d, -1).wait_send()

                if k < plain:
                    y_copy(k, f + d, g).wait_send()

    def finish(o, total):
        origin, copy = take(o)
        copy.wait_recv()
        return total + gath[origin]

    total = lax.fori_loop(1, n, finish, part[me])
    out[0] = total[:, :2 * ki] * lax.rsqrt(total[:, 2 * ki:2 * ki + 1] * 0.25)

    def drain(o, carry):
        give(o).wait_send()
        return carry

    lax.fori_loop(1, n, drain, 0)


def body(
    patches, cotangent, segment, home_map, ln_gain, w_up, w_down_t, p_in1, q_out1, p_in2, q_out2
):
    fn, sn = lax.axis_size("fsdp"), lax.axis_size("seq")
    n = fn * sn * 2
    rows, width = patches.shape
    cols = w_up.shape[1] // 2
    chunks = cols // KC
    extra = 1 if fn == 4 else 0
    blocks = 2 + 2 * extra
    steps = chunks + extra
    ko, ki = q_out1.shape[1], p_in1.shape[1]
    any_ = pl.BlockSpec(memory_space=pltpu.HBM)
    vmem = pl.BlockSpec(memory_space=pltpu.VMEM)
    smem = pl.BlockSpec(memory_space=pltpu.SMEM)
    dma = pltpu.SemaphoreType.DMA
    return pl.pallas_call(
        functools.partial(kernel, fn, sn, chunks, extra),
        out_shape=jax.ShapeDtypeStruct((1, ko // 2, 2 * ki), F32),
        in_specs=[any_, any_, vmem, smem, vmem, any_, any_, any_, any_, any_, any_],
        out_specs=vmem,
        scratch_shapes=[
            pltpu.VMEM((rows, width), BF),
            pltpu.VMEM((2, blocks * rows, width), BF),
            pltpu.VMEM((blocks, 8, rows), jnp.int32),
            pltpu.VMEM((chunks, 2, 2, width, HC), BF),
            pltpu.VMEM((128, width), BF),
            pltpu.VMEM((128, cols), BF),
            pltpu.VMEM((ko, cols), BF),
            pltpu.VMEM((ko, width), BF),
            pltpu.VMEM((blocks, rows, 128), F32),
            pltpu.VMEM((blocks, rows, 128), F32),
            pltpu.VMEM((blocks, ko, rows), F32),
            pltpu.VMEM((blocks, ko, rows), F32),
            pltpu.VMEM((n, ko // 2, 128), F32),
            pltpu.VMEM((n, ko // 2, 128), F32),
            dma((6,)),
            dma((chunks, 2, 2)),
            dma((steps, fn)),
            dma((steps, fn)),
            dma((steps, fn)),
            dma((steps, fn)),
            dma((steps, fn)),
            dma((2, 2, blocks)),
            dma((2, 2)),
            dma((2, 2, blocks)),
            dma((2, blocks)),
            dma((n,)),
            dma((n,)),
        ],
        compiler_params=pltpu.CompilerParams(
            collective_id=0, has_side_effects=True, vmem_limit_bytes=63 * 1024 * 1024
        ),
    )(
        patches, cotangent, segment, home_map, ln_gain,
        w_up, w_down_t, p_in1.T, q_out1.T, p_in2.T, q_out2.T,
    )


def solution(mesh):
    return jax.shard_map(
        body,
        mesh=mesh,
        in_specs=(
            P(("group", "fsdp", "seq"), None),
            P(("group", "fsdp", "seq"), None),
            P(("group", "fsdp", "seq")),
            P("group"),
            P(),
            P("fsdp", "proj"),
            P("fsdp", "proj"),
            P(),
            P("proj", None),
            P("proj", None),
            P(),
        ),
        out_specs=P(("group", "fsdp", "seq"), "proj", None),
        check_vma=False,
    )
```

```python
import functools

import jax
import jax.numpy as jnp
from jax import lax
from jax.experimental import pallas as pl
from jax.experimental.pallas import tpu as pltpu
from jax.sharding import PartitionSpec as P

KC = 256
HC = 128
MESH = pl.DeviceIdType.MESH
BF = jnp.bfloat16
F32 = jnp.float32
NT = (((1,), (1,)), ((), ()))


def kernel(
    fn, sn, chunks, extra,
    patches, cot, seg, home, gain, w_up, w_down, p_in1, q_out1, p_in2, q_out2,
    out,
    pbuf, xbuf, sbuf, wbuf, p1p, p2p, q1t, q2t, in1, in2, t1, t2, part, gath,
    lsem, wsem, zrecv, yrecv, rsend, lsend, ysend, xsem, esem, csem, seg_sem, red_send, red_recv,
):
    g, f = lax.axis_index("group"), lax.axis_index("fsdp")
    s, p = lax.axis_index("seq"), lax.axis_index("proj")
    s2 = lax.rem(s, 2)
    mate = s + 1 - 2 * s2
    n = fn * sn * 2
    me = (f * sn + s) * 2 + p
    rows, width = patches.shape
    half = rows // 2
    depth = w_up.shape[0]
    images = home.shape[0]
    ko = q_out1.shape[0]
    ki = p_in1.shape[0]
    cols = chunks * KC
    base = pl.multiple_of(s2 * cols, KC)

    def spot(linear):
        return {"fsdp": linear // (2 * sn), "seq": lax.rem(linear // 2, sn), "proj": lax.rem(linear, 2)}

    barrier = pltpu.get_barrier_semaphore()

    def greet(o, carry):
        pl.semaphore_signal(barrier, inc=1, device_id=spot(lax.rem(me + o, n)), device_id_type=MESH)
        return carry

    lax.fori_loop(1, n, greet, 0)
    pl.semaphore_signal(barrier, inc=1, device_id={"group": 1 - g}, device_id_type=MESH)

    own_rows = pl.ds(0, rows)
    loads = [
        pltpu.make_async_copy(patches, pbuf, lsem.at[0]),
        pltpu.make_async_copy(cot, xbuf.at[1, own_rows], lsem.at[1]),
        pltpu.make_async_copy(q_out1.at[:, pl.ds(base, cols)], q1t, lsem.at[2]),
        pltpu.make_async_copy(p_in2.at[:, pl.ds(base, cols)], p2p.at[pl.ds(ki, ki)], lsem.at[3]),
        pltpu.make_async_copy(p_in1, p1p.at[pl.ds(0, ki)], lsem.at[4]),
        pltpu.make_async_copy(q_out2, q2t, lsem.at[5]),
    ]

    p1p[ki:, :] = jnp.zeros((128 - ki, width), BF)
    p2p[:ki, :] = jnp.zeros((ki, cols), BF)
    p2p[2 * ki:, :] = jnp.zeros((128 - 2 * ki, cols), BF)

    def own_load(k, m, side):
        source = (w_up, w_down)[m]
        columns = pl.ds(pl.multiple_of(base + k * KC + side * HC, HC), HC)
        return pltpu.make_async_copy(
            source.at[:, columns], wbuf.at[k, side, m, pl.ds(pl.multiple_of(f * depth, depth), depth)],
            wsem.at[k, m, side],
        )

    for k in range(chunks):
        for m in range(2):
            for side in range(2):
                own_load(k, m, side).start()
        if k == 0:
            loads[1].start()
            loads[0].start()
    for load in loads[2:]:
        load.start()
    plain = chunks - extra
    middle = jnp.logical_and(f >= 1, f <= fn - 2)
    end = jnp.logical_not(middle)
    sbuf[0] = jnp.broadcast_to(seg[...].reshape(1, rows), sbuf.shape[1:])

    pl.semaphore_wait(barrier, n)

    steps = plain + 2 * extra

    def piece(k, source, side):
        at = pl.ds(pl.multiple_of(source * depth, depth), depth)
        if k < plain:
            return wbuf.at[k, side, :, at]
        return wbuf.at[plain, k - plain, :, at]

    def z_copy(k, source, way):
        sems = rsend if way > 0 else lsend
        block = piece(k, source, g)
        return pltpu.make_async_remote_copy(
            src_ref=block, dst_ref=block, send_sem=sems.at[k, source], recv_sem=zrecv.at[k, source],
            device_id={"fsdp": f + way}, device_id_type=MESH,
        )

    def y_copy(k, source, side):
        block = piece(k, source, side)
        return pltpu.make_async_remote_copy(
            src_ref=block, dst_ref=block, send_sem=ysend.at[k, source], recv_sem=yrecv.at[k, source],
            device_id={"group": 1 - g}, device_id_type=MESH,
        )

    def to_right(k):
        return f < (fn - 1 if k < plain else fn - 2)

    def to_left(k):
        return f > (0 if k < plain else 1)

    def got(k, d):
        left, right = f - d >= 0, f + d < fn
        if k >= plain:
            left, right = jnp.logical_and(left, middle), jnp.logical_and(right, middle)
        return left, right

    def send_own(k):
        if k < plain or k == plain:
            for m in range(2):
                for side in range(2):
                    own_load(min(k, plain), m, side).wait()

        @pl.when(to_right(k))
        def _():
            z_copy(k, f, 1).start()

        @pl.when(to_left(k))
        def _():
            z_copy(k, f, -1).start()

    def forward(k):
        for d in range(1, fn):
            left, right = got(k, d)

            @pl.when(left)
            def _():
                z_copy(k, f - d, 1).wait_recv()

                @pl.when(to_right(k))
                def _():
                    z_copy(k, f - d, 1).start()

                if k < plain:
                    y_copy(k, f - d, g).start()

            @pl.when(right)
            def _():
                z_copy(k, f + d, -1).wait_recv()

                @pl.when(to_left(k))
                def _():
                    z_copy(k, f + d, -1).start()

                if k < plain:
                    y_copy(k, f + d, g).start()

    def half_of(m, block, side):
        return xbuf.at[m, pl.ds(pl.multiple_of(block * rows + side * half, half), half)]

    def x_copy(m, block):
        return pltpu.make_async_remote_copy(
            src_ref=half_of(m, block, p), dst_ref=half_of(m, block + 1, p),
            send_sem=xsem.at[0, m, block], recv_sem=xsem.at[1, m, block],
            device_id={"seq": mate}, device_id_type=MESH,
        )

    def c_copy(m, block, side):
        return pltpu.make_async_remote_copy(
            src_ref=half_of(m, block, side), dst_ref=half_of(m, block, side),
            send_sem=csem.at[0, m, block], recv_sem=csem.at[1, m, block],
            device_id={"proj": 1 - p}, device_id_type=MESH,
        )

    inward = jnp.where(f == 0, 1, fn - 2)

    def e_copy(m):
        return pltpu.make_async_remote_copy(
            src_ref=half_of(m, 0, p), dst_ref=half_of(m, 2, p), send_sem=esem.at[0, m], recv_sem=esem.at[1, m],
            device_id={"fsdp": inward}, device_id_type=MESH,
        )

    def seg_copy(source, target, where):
        return pltpu.make_async_remote_copy(
            src_ref=sbuf.at[source], dst_ref=sbuf.at[target], send_sem=seg_sem.at[0, target],
            recv_sem=seg_sem.at[1, target], device_id=where, device_id_type=MESH,
        )

    across = {"seq": mate}
    loads[1].wait()
    x_copy(1, 0).start()
    seg_copy(0, 1, across).start()
    if extra:
        @pl.when(end)
        def _():
            e_copy(1).start()
            seg_copy(0, 2, {"fsdp": inward}).start()

    send_own(0)
    loads[0].wait()
    step = 32
    scale = gain[...].reshape(1, width)

    def norm(i, carry):
        at = pl.ds(pl.multiple_of(i * step, step), step)
        values = pbuf[at, :].astype(F32)
        center = values - jnp.mean(values, axis=-1, keepdims=True)
        spread = jnp.mean(center * center, axis=-1, keepdims=True)
        xbuf[0, at, :] = (center * lax.rsqrt(spread + 1e-06) * scale).astype(BF)
        return carry

    lax.fori_loop(0, rows // step, norm, 0)
    x_copy(0, 0).start()
    if extra:
        @pl.when(end)
        def _():
            e_copy(0).start()

    send_own(1)
    for load in loads[2:]:
        load.wait()

    def small(r):
        at = pl.ds(r * rows, rows)
        in1[r] = lax.dot_general(xbuf[0, at, :], p1p[...], NT, preferred_element_type=F32)
        t2[r] = lax.dot_general(q2t[...], xbuf[1, at, :], NT, preferred_element_type=F32)

    def compute(k, low, high):
        for d in range(1, fn if k < plain else 1):
            @pl.when(f - d >= 0)
            def _():
                y_copy(k, f - d, 1 - g).wait_recv()

            @pl.when(f + d < fn)
            def _():
                y_copy(k, f + d, 1 - g).wait_recv()

        def rows_of(r, carry):
            at = pl.ds(pl.multiple_of(r * rows, rows), rows)
            up = jnp.concatenate([wbuf[k, 0, 0], wbuf[k, 1, 0]], axis=1)
            down = jnp.concatenate([wbuf[k, 0, 1], wbuf[k, 1, 1]], axis=1)
            pre = jnp.dot(xbuf[0, at, :], up, preferred_element_type=F32)
            dact = jnp.dot(xbuf[1, at, :], down, preferred_element_type=F32)
            sigma = 0.5 + 0.5 * jnp.tanh(0.851 * pre)
            act = (pre * sigma).astype(BF)
            dpre = (dact * (sigma * (1.0 + 1.702 * pre * (1.0 - sigma)))).astype(BF)
            two = lax.dot_general(act, p2p[:, k * KC:(k + 1) * KC], NT, preferred_element_type=F32)
            one = lax.dot_general(q1t[:, k * KC:(k + 1) * KC], dpre, NT, preferred_element_type=F32)
            if k == 0 or low >= 2:
                in2[r] = two
                t1[r] = one
            else:
                in2[r] += two
                t1[r] += one
            return carry

        lax.fori_loop(low, high, rows_of, 0)

    def hand_on(m, block):
        c_copy(m, block, p).start()

    def from_end(m):
        if extra:
            @pl.when(middle)
            def _():
                e_copy(m).wait_recv()
                x_copy(m, 2).start()
                hand_on(m, 2)

    small(0)
    forward(0)
    send_own(2)
    forward(1)
    send_own(3)
    x_copy(1, 0).wait_recv()
    hand_on(1, 1)
    from_end(1)
    x_copy(0, 0).wait_recv()
    hand_on(0, 1)
    seg_copy(0, 1, across).wait_recv()
    c_copy(1, 1, 1 - p).wait_recv()
    c_copy(0, 1, 1 - p).wait_recv()
    if extra:
        @pl.when(middle)
        def _():
            seg_copy(0, 2, {"fsdp": inward}).wait_recv()
            seg_copy(2, 3, across).start()

    small(1)
    for k in range(2, steps):
        if k == 2:
            from_end(0)
        forward(k)
        if k + 2 < steps:
            send_own(k + 2)
        if k - 2 < plain - 1:
            compute(k - 2, 0, 2)
    for k in range(steps - 2, plain):
        compute(k, 0, 2)
    if extra:
        compute(plain - 1, 0, 2)

        @pl.when(middle)
        def _():
            for m in (1, 0):
                c_copy(m, 2, 1 - p).wait_recv()
            small(2)
            for m in (1, 0):
                x_copy(m, 2).wait_recv()
                hand_on(m, 3)
            compute(plain, 0, 2)
            compute(plain, 2, 3)
            seg_copy(2, 3, across).wait_recv()
            for m in (1, 0):
                c_copy(m, 3, 1 - p).wait_recv()
            small(3)
            compute(plain, 3, 4)

    lane = lax.broadcasted_iota(jnp.int32, (ko // 2, 128), 1)
    many = 8

    def blocks(b, carry):
        def add(r, sums):
            raw, counts = sums
            ids = sbuf[r, 0:1, :]
            goal = lax.fori_loop(
                0, images, lambda e, t: jnp.where(ids == e, home[e], t), jnp.zeros_like(ids), unroll=images <= 8
            )
            marks = [(goal == b * many + j).astype(F32) for j in range(many)]
            own = (r < 2).astype(F32)
            counts = tuple(c + own * jnp.sum(m, axis=1, keepdims=True) for c, m in zip(counts, marks))
            left1 = jnp.concatenate([t1[r] * m for m in marks], axis=0)
            left2 = jnp.concatenate([t2[r] * m for m in marks], axis=0)
            raw += jnp.dot(left1, in1[r], preferred_element_type=F32, precision=lax.Precision.HIGHEST)
            raw += jnp.dot(left2, in2[r], preferred_element_type=F32, precision=lax.Precision.HIGHEST)
            return raw, counts

        blank = (jnp.zeros((many * ko, 128), F32), (jnp.zeros((1, 1), F32),) * many)
        raw, counts = lax.fori_loop(0, jnp.where(middle, 4, 2) if extra else 2, add, blank)
        for j in range(many):
            for c in range(2):
                start = j * ko + c * (ko // 2)
                part[(b * many + j) * 2 + c] = jnp.where(
                    lane == 2 * ki, counts[j], raw[start:start + ko // 2]
                )
        return carry

    lax.fori_loop(0, images // many, blocks, 0)

    def give(o):
        target = lax.rem(me + o, n)
        return pltpu.make_async_remote_copy(
            src_ref=part.at[target], dst_ref=gath.at[me], send_sem=red_send.at[target], recv_sem=red_recv.at[me],
            device_id=spot(target), device_id_type=MESH,
        )

    def take(o):
        origin = lax.rem(me + n - o, n)
        return origin, pltpu.make_async_remote_copy(
            src_ref=part.at[origin], dst_ref=gath.at[origin], send_sem=red_send.at[origin],
            recv_sem=red_recv.at[origin], device_id=spot(origin), device_id_type=MESH,
        )

    def start(o, carry):
        give(o).start()
        return carry

    lax.fori_loop(1, n, start, 0)

    for m in range(2):
        x_copy(m, 0).wait_send()
        c_copy(m, 1, p).wait_send()
    seg_copy(0, 1, across).wait_send()
    if extra:
        @pl.when(end)
        def _():
            for m in range(2):
                e_copy(m).wait_send()
            seg_copy(0, 2, {"fsdp": inward}).wait_send()

        @pl.when(middle)
        def _():
            for m in range(2):
                x_copy(m, 2).wait_send()
                c_copy(m, 2, p).wait_send()
                c_copy(m, 3, p).wait_send()
            seg_copy(2, 3, across).wait_send()

    for k in range(steps):
        @pl.when(to_right(k))
        def _():
            z_copy(k, f, 1).wait_send()

        @pl.when(to_left(k))
        def _():
            z_copy(k, f, -1).wait_send()

        for d in range(1, fn):
            left, right = got(k, d)

            @pl.when(left)
            def _():
                @pl.when(to_right(k))
                def _():
                    z_copy(k, f - d, 1).wait_send()

                if k < plain:
                    y_copy(k, f - d, g).wait_send()

            @pl.when(right)
            def _():
                @pl.when(to_left(k))
                def _():
                    z_copy(k, f + d, -1).wait_send()

                if k < plain:
                    y_copy(k, f + d, g).wait_send()

    def finish(o, total):
        origin, copy = take(o)
        copy.wait_recv()
        return total + gath[origin]

    total = lax.fori_loop(1, n, finish, part[me])
    out[0] = total[:, :2 * ki] * lax.rsqrt(total[:, 2 * ki:2 * ki + 1] * 0.25)

    def drain(o, carry):
        give(o).wait_send()
        return carry

    lax.fori_loop(1, n, drain, 0)


def body(
    patches, cotangent, segment, home_map, ln_gain, w_up, w_down_t, p_in1, q_out1, p_in2, q_out2
):
    fn, sn = lax.axis_size("fsdp"), lax.axis_size("seq")
    n = fn * sn * 2
    rows, width = patches.shape
    cols = w_up.shape[1] // 2
    chunks = cols // KC
    extra = 1 if fn == 4 else 0
    blocks = 2 + 2 * extra
    steps = chunks + extra
    ko, ki = q_out1.shape[1], p_in1.shape[1]
    any_ = pl.BlockSpec(memory_space=pltpu.HBM)
    vmem = pl.BlockSpec(memory_space=pltpu.VMEM)
    smem = pl.BlockSpec(memory_space=pltpu.SMEM)
    dma = pltpu.SemaphoreType.DMA
    return pl.pallas_call(
        functools.partial(kernel, fn, sn, chunks, extra),
        out_shape=jax.ShapeDtypeStruct((1, ko // 2, 2 * ki), F32),
        in_specs=[any_, any_, vmem, smem, vmem, any_, any_, any_, any_, any_, any_],
        out_specs=vmem,
        scratch_shapes=[
            pltpu.VMEM((rows, width), BF),
            pltpu.VMEM((2, blocks * rows, width), BF),
            pltpu.VMEM((blocks, 8, rows), jnp.int32),
            pltpu.VMEM((chunks, 2, 2, width, HC), BF),
            pltpu.VMEM((128, width), BF),
            pltpu.VMEM((128, cols), BF),
            pltpu.VMEM((ko, cols), BF),
            pltpu.VMEM((ko, width), BF),
            pltpu.VMEM((blocks, rows, 128), F32),
            pltpu.VMEM((blocks, rows, 128), F32),
            pltpu.VMEM((blocks, ko, rows), F32),
            pltpu.VMEM((blocks, ko, rows), F32),
            pltpu.VMEM((n, ko // 2, 128), F32),
            pltpu.VMEM((n, ko // 2, 128), F32),
            dma((6,)),
            dma((chunks, 2, 2)),
            dma((steps, fn)),
            dma((steps, fn)),
            dma((steps, fn)),
            dma((steps, fn)),
            dma((steps, fn)),
            dma((2, 2, blocks)),
            dma((2, 2)),
            dma((2, 2, blocks)),
            dma((2, blocks)),
            dma((n,)),
            dma((n,)),
        ],
        compiler_params=pltpu.CompilerParams(
            collective_id=0, has_side_effects=True, vmem_limit_bytes=63 * 1024 * 1024
        ),
    )(
        patches, cotangent, segment, home_map, ln_gain,
        w_up, w_down_t, p_in1.T, q_out1.T, p_in2.T, q_out2.T,
    )


def solution(mesh):
    return jax.shard_map(
        body,
        mesh=mesh,
        in_specs=(
            P(("group", "fsdp", "seq"), None),
            P(("group", "fsdp", "seq"), None),
            P(("group", "fsdp", "seq")),
            P("group"),
            P(),
            P("fsdp", "proj"),
            P("fsdp", "proj"),
            P(),
            P("proj", None),
            P("proj", None),
            P(),
        ),
        out_specs=P(("group", "fsdp", "seq"), "proj", None),
        check_vma=False,
    )
```
